128 devices in a mesh: dp: 8 (over y_lo, z), mp: 16 (over x, y_hi, core).
Axes of the slice: x: 4, y: 4 (y_hi: 2, y_lo: 2; y = y_hi * 2 + y_lo), z: 4, core: 2. Of those that a mesh axis runs over, the one named last changes fastest.
Arguments:
- tokens: bfloat16 [128, 256, 1280], P(('dp', 'mp'))
- slot_keys: bfloat16 [256, 1280], P(('dp', 'mp'))
- weight_in: bfloat16 [128, 1280, 2560], P(('dp', 'mp')), may hold values from -0.15625 to 0.15625
- weight_out: bfloat16 [128, 2560, 1280], P(('dp', 'mp')), may hold values from -0.125 to 0.125
- cotangent: bfloat16 [128, 256, 1280], P(('dp', 'mp')), may hold values from -6 to 6
Outputs:
- mixed_out: bfloat16 [128, 256, 1280], P(('dp', 'mp'))
- grad_tokens: bfloat16 [128, 256, 1280], P(('dp', 'mp'))
- grad_keys: float32 [256, 1280], P(('dp', 'mp'))
- grad_w_out: bfloat16 [128, 2560, 1280], P(('dp', 'mp'))
The draws below stay inside these ranges and needn't reach their ends.
All inputs are finite; a program needn't handle non-finite values.
Results may differ from the reference program's by a relative error of at most 0.01.
Values may be sent and summed in bfloat16 or wider, within the bound.
No kernel may reach another device: no remote copies, remote signals or barrier semaphores. Data moves between devices by JAX's collectives and lax.ppermute only.
A program may use at most 128 MiB of HBM per device.

```python
import math
import jax
import jax.numpy as jnp
from jax import lax

D = 1280
FF = 2560
TOK_IMG = 256
SLOTS_EXP = 2
EXPERTS = 128
SLOTS = 256
IMAGES = 128


def joint_draw(key):
    folded = jax.random.fold_in(key, 17)
    streams = jax.random.split(folded, 6)
    spread_scale = 3.0 / math.sqrt(D)
    slot_keys = jnp.clip(jax.random.normal(streams[0], (SLOTS, D), jnp.float32), -6.0, 6.0) * spread_scale
    tokens = jnp.clip(jax.random.normal(streams[5], (IMAGES, TOK_IMG, D), jnp.float32), -6.0, 6.0)
    return (tokens, slot_keys)


def draw_tokens(key, part):
    return joint_draw(key)[0].astype(jnp.bfloat16)


def draw_slot_keys(key, part):
    return joint_draw(key)[1].astype(jnp.bfloat16)


def level_of(stream_key, shape, cuts, smallest, largest):
    def one(position, parts):
        draws = jax.random.uniform(jax.random.fold_in(jax.random.fold_in(stream_key, 6), position), (parts,), jnp.float32, smallest / len(cuts), largest / len(cuts))
        return jnp.repeat(jnp.exp(draws), shape[position] // parts).reshape((-1,) + (1,) * (len(shape) - position - 1))

    loudness = one(*cuts[0])
    for cut in cuts[1:]:
        loudness = loudness * one(*cut)
    return loudness


def gaussian(rng, shape, scale, most, shards=(), kind=jnp.bfloat16):
    factor_of = level_of(rng, shape, shards, -0.22, 0.18) if shards else 1.0
    entries = jax.random.normal(rng, shape, jnp.float32) * scale * factor_of
    return jnp.minimum(jnp.maximum(entries, -most), most).astype(kind)


def setup_inputs(seed: int = 0) -> dict:
    seeds = jax.random.split(jax.random.key(seed), 6)
    return {
        "tokens": draw_tokens(jax.random.fold_in(seeds[5], 71), 0),
        "slot_keys": draw_slot_keys(jax.random.fold_in(seeds[5], 71), 0),
        "weight_in": gaussian(seeds[2], (EXPERTS, D, FF), D ** -0.5, 0.15625, ((0, 128),)),
        "weight_out": gaussian(seeds[3], (EXPERTS, FF, D), FF ** -0.5, 0.125, ((0, 128),)),
        "cotangent": gaussian(seeds[4], (IMAGES, TOK_IMG, D), 1.0, 6.0, ((0, 128),)),
    }


inv_root_two = 0.7071067811865476
inv_root_tau = 0.3989422804014327


def gelu_pair(values):
    cumulative = 0.5 * (1.0 + jax.scipy.special.erf(values * inv_root_two))
    density = jnp.exp(-0.5 * values * values) * inv_root_tau
    return values * cumulative, cumulative + values * density


def to_experts(per_image):
    shaped = per_image.reshape(IMAGES, EXPERTS, SLOTS_EXP, D)
    return shaped.transpose(1, 0, 2, 3).reshape(EXPERTS, IMAGES * SLOTS_EXP, D)


def to_images(per_expert):
    shaped = per_expert.reshape(EXPERTS, IMAGES, SLOTS_EXP, D)
    return shaped.transpose(1, 0, 2, 3).reshape(IMAGES, SLOTS, D)


def reference(tokens, slot_keys, weight_in, weight_out, cotangent):
    def image_logits(image_rows):
        return jnp.dot(image_rows, slot_keys.T, preferred_element_type=jnp.float32)

    def image_slots(image_rows):
        dispatch = jax.nn.softmax(image_logits(image_rows), axis=0)
        dispatch_low = dispatch.astype(jnp.bfloat16)
        return jnp.dot(dispatch_low.T, image_rows, preferred_element_type=jnp.float32).astype(jnp.bfloat16)

    slots_in = lax.map(image_slots, tokens)
    expert_rows = to_experts(slots_in)

    def expert_forward(inputs):
        slot_rows, first, second = inputs
        pre_act = jnp.dot(slot_rows, first, preferred_element_type=jnp.float32)
        hidden = gelu_pair(pre_act)[0].astype(jnp.bfloat16)
        return jnp.dot(hidden, second, preferred_element_type=jnp.float32).astype(jnp.bfloat16)

    slot_out = to_images(lax.map(expert_forward, (expert_rows, weight_in, weight_out)))

    def image_combine(inputs):
        image_rows, outputs, grad_out = inputs
        combine = jax.nn.softmax(image_logits(image_rows), axis=1)
        combine_low = combine.astype(jnp.bfloat16)
        mixed_out = jnp.dot(combine_low, outputs, preferred_element_type=jnp.float32).astype(jnp.bfloat16)
        grad_slots = jnp.dot(combine_low.T, grad_out, preferred_element_type=jnp.float32).astype(jnp.bfloat16)
        return mixed_out, grad_slots

    mixed_out, grad_slot_out = lax.map(image_combine, (tokens, slot_out, cotangent))

    def expert_backward(inputs):
        slot_rows, grad_rows, first, second = inputs
        pre_act = jnp.dot(slot_rows, first, preferred_element_type=jnp.float32)
        active, gelu_slope = gelu_pair(pre_act)
        hidden = active.astype(jnp.bfloat16)
        grad_second = jnp.dot(hidden.T, grad_rows, preferred_element_type=jnp.float32).astype(jnp.bfloat16)
        grad_hidden = jnp.dot(grad_rows, second.T, preferred_element_type=jnp.float32)
        grad_pre = (grad_hidden * gelu_slope).astype(jnp.bfloat16)
        grad_rows_in = jnp.dot(grad_pre, first.T, preferred_element_type=jnp.float32).astype(jnp.bfloat16)
        return grad_rows_in, grad_second

    grad_rows_in, grad_w_out = lax.map(expert_backward, (expert_rows, to_experts(grad_slot_out), weight_in, weight_out))
    grad_slot_in = to_images(grad_rows_in)

    def image_backward(key_total, inputs):
        image_rows, outputs, grad_out, grad_in = inputs
        logits = image_logits(image_rows)
        dispatch = jax.nn.softmax(logits, axis=0)
        combine = jax.nn.softmax(logits, axis=1)
        dispatch_low = dispatch.astype(jnp.bfloat16)
        grad_combine = jnp.dot(grad_out, outputs.T, preferred_element_type=jnp.float32)
        grad_dispatch = jnp.dot(image_rows, grad_in.T, preferred_element_type=jnp.float32)
        grad_logits = dispatch * (grad_dispatch - jnp.sum(dispatch * grad_dispatch, axis=0, keepdims=True)) + combine * (grad_combine - jnp.sum(combine * grad_combine, axis=1, keepdims=True))
        grad_low = grad_logits.astype(jnp.bfloat16)
        through_slots = jnp.dot(dispatch_low, grad_in, preferred_element_type=jnp.float32)
        through_keys = jnp.dot(grad_low, slot_keys, preferred_element_type=jnp.float32)
        grad_image = (through_slots + through_keys).astype(jnp.bfloat16)
        key_total = key_total + jnp.dot(grad_low.T, image_rows, preferred_element_type=jnp.float32)
        return key_total, grad_image

    grad_keys, grad_tokens = lax.scan(image_backward, jnp.zeros((SLOTS, D), jnp.float32), (tokens, slot_out, cotangent, grad_slot_in))
    return (mixed_out, grad_tokens, grad_keys, grad_w_out)
```

```python
import jax
import jax.numpy as jnp
from jax import lax
from jax.sharding import PartitionSpec as P

SLOTS_EXP = 2
AXES = ("dp", "mp")

inv_root_two = 0.7071067811865476
inv_root_tau = 0.3989422804014327


def gelu_pair(values):
    cumulative = 0.5 * (1.0 + jax.scipy.special.erf(values * inv_root_two))
    density = jnp.exp(-0.5 * values * values) * inv_root_tau
    return (values * cumulative, cumulative + values * density)


def exchange(blocks):
    return lax.all_to_all(blocks, AXES, split_axis=0, concat_axis=0, tiled=True)


def dot(a, b, dims):
    return lax.dot_general(a, b, (dims, ((), ())), preferred_element_type=jnp.float32)


def local(tokens, slot_keys, weight_in, weight_out, cotangent):
    low = jnp.bfloat16
    devices = lax.axis_size(AXES)
    length, width = tokens.shape[1:]
    tokens, cotangent = tokens[0], cotangent[0]
    first_weight, second_weight = weight_in[0], weight_out[0]
    keys_all = exchange(jnp.broadcast_to(slot_keys[None], (devices, SLOTS_EXP, width)))
    keys_all = keys_all.reshape(-1, width)
    slots = keys_all.shape[0]

    logits = dot(tokens, keys_all, ((1,), (1,)))
    dispatch = jax.nn.softmax(logits, axis=0)
    combine = jax.nn.softmax(logits, axis=1)
    dispatch_low = dispatch.astype(low)
    combine_low = combine.astype(low)
    slots_in = dot(dispatch_low, tokens, ((0,), (0,))).astype(low)
    grad_slot_out = dot(combine_low, cotangent, ((0,), (0,))).astype(low)
    parts = (devices, SLOTS_EXP, width)
    arrived = exchange(
        jnp.concatenate([slots_in.reshape(parts), grad_slot_out.reshape(parts)], axis=1)
    )
    slot_rows = arrived[:, :SLOTS_EXP].reshape(-1, width)
    grad_rows = arrived[:, SLOTS_EXP:].reshape(-1, width)

    pre_act = dot(slot_rows, first_weight, ((1,), (0,)))
    active, gelu_slope = gelu_pair(pre_act)
    hidden = active.astype(low)
    expert_out = dot(hidden, second_weight, ((1,), (0,))).astype(low)
    grad_hidden = dot(grad_rows, second_weight, ((1,), (1,)))
    grad_pre = (grad_hidden * gelu_slope).astype(low)
    grad_rows_in = dot(grad_pre, first_weight, ((1,), (1,))).astype(low)
    back = exchange(
        jnp.concatenate([expert_out.reshape(parts), grad_rows_in.reshape(parts)], axis=1)
    )
    grad_second = dot(hidden, grad_rows, ((0,), (0,))).astype(low)
    slot_out = back[:, :SLOTS_EXP].reshape(slots, width)
    grad_slot_in = back[:, SLOTS_EXP:].reshape(slots, width)

    grad_combine = dot(cotangent, slot_out, ((1,), (1,)))
    grad_dispatch = dot(tokens, grad_slot_in, ((1,), (1,)))
    grad_logits = dispatch * (
        grad_dispatch - jnp.sum(dispatch * grad_dispatch, axis=0, keepdims=True)
    ) + combine * (grad_combine - jnp.sum(combine * grad_combine, axis=1, keepdims=True))
    grad_low = grad_logits.astype(low)
    key_terms = dot(grad_low, tokens, ((0,), (0,))).astype(low)
    key_parts = exchange(key_terms.reshape(parts))
    mixed_out = dot(combine_low, slot_out, ((1,), (0,))).astype(low)
    through_slots = dot(dispatch_low, grad_slot_in, ((1,), (0,)))
    through_keys = dot(grad_low, keys_all, ((1,), (0,)))
    grad_tokens = (through_slots + through_keys).astype(low)
    grad_keys = jnp.sum(key_parts.astype(jnp.float32), axis=0)
    return (mixed_out[None], grad_tokens[None], grad_keys, grad_second[None])


def solution(mesh):
    in_specs = (
        P(AXES, None, None),
        P(AXES, None),
        P(AXES, None, None),
        P(AXES, None, None),
        P(AXES, None, None),
    )
    out_specs = (
        P(AXES, None, None),
        P(AXES, None, None),
        P(AXES, None),
        P(AXES, None, None),
    )
    return jax.shard_map(local, mesh=mesh, in_specs=in_specs, out_specs=out_specs, check_vma=False)
```

```python
import jax
import jax.numpy as jnp
from jax import lax
from jax.experimental import pallas as pl
from jax.experimental.pallas import tpu as pltpu
from jax.sharding import PartitionSpec as P

SLOTS_EXP = 2
AXES = ("dp", "mp")
LOW = jnp.bfloat16
FF_BLOCK = 512
D_BLOCK = 256
MIB = 1 << 20

inv_root_two = 0.7071067811865476
inv_root_tau = 0.3989422804014327


def gelu_pair(values):
    cumulative = 0.5 * (1.0 + lax.erf(values * inv_root_two))
    density = jnp.exp(-0.5 * values * values) * inv_root_tau
    return (values * cumulative, cumulative + values * density)


def device_count():
    return lax.axis_size(AXES)


def exchange(blocks):
    return lax.all_to_all(blocks, AXES, split_axis=0, concat_axis=0, tiled=True)


def dot(a, b, dims):
    return lax.dot_general(a, b, (dims, ((), ())), preferred_element_type=jnp.float32)


def softmax(values, axis):
    powers = jnp.exp(values - jnp.max(values, axis=axis, keepdims=True))
    return powers / jnp.sum(powers, axis=axis, keepdims=True)


def route_kernel(tokens, cotangent, keys, send, dispatch_out, combine_out, keys_out):
    pairs = keys.shape[0]
    slots, width = keys_out.shape
    keys_out[...] = keys[...].reshape(slots, width)
    logits = dot(tokens[...], keys_out[...], ((1,), (1,)))
    dispatch = softmax(logits, 0)
    dispatch_out[...] = dispatch
    slots_in = dot(dispatch.astype(LOW), tokens[...], ((0,), (0,))).astype(LOW)
    send[:, 0] = slots_in.reshape(pairs, SLOTS_EXP, width)
    combine = softmax(logits, 1)
    combine_out[...] = combine
    grad_slot_out = dot(combine.astype(LOW), cotangent[...], ((0,), (0,))).astype(LOW)
    send[:, 1] = grad_slot_out.reshape(pairs, SLOTS_EXP, width)


def expert_kernel(
    arrived, first_hbm, second_hbm, send, hidden, grads, rows, grad_pre, first, second, sems
):
    width, inner = first.shape
    pairs = arrived.shape[0]
    steps = inner // FF_BLOCK
    copies = []
    for i in range(steps):
        block = pl.ds(i * FF_BLOCK, FF_BLOCK)
        copies.append(
            (
                pltpu.make_async_copy(first_hbm.at[:, block], first.at[:, block], sems.at[0, i]),
                pltpu.make_async_copy(second_hbm.at[block, :], second.at[block, :], sems.at[1, i]),
            )
        )
    for copy_in, copy_out in copies:
        copy_in.start()
        copy_out.start()
    rows[...] = arrived[:, 0].reshape(rows.shape)
    grads[...] = arrived[:, 1].reshape(rows.shape)
    for i in range(steps):
        block = pl.ds(i * FF_BLOCK, FF_BLOCK)
        copies[i][0].wait()
        pre_act = dot(rows[...], first[:, block], ((1,), (0,)))
        copies[i][1].wait()
        grad_hidden = dot(grads[...], second[block, :], ((1,), (1,)))
        active, slope = gelu_pair(pre_act)
        hidden[:, block] = active.astype(LOW)
        grad_pre[:, block] = (grad_hidden * slope).astype(LOW)
    for j in range(width // D_BLOCK):
        block = pl.ds(j * D_BLOCK, D_BLOCK)
        out = dot(hidden[...], second[:, block], ((1,), (0,))).astype(LOW)
        send[:, 0, :, block] = out.reshape(pairs, SLOTS_EXP, D_BLOCK)
        back = dot(grad_pre[...], first[block, :], ((1,), (1,))).astype(LOW)
        send[:, 1, :, block] = back.reshape(pairs, SLOTS_EXP, D_BLOCK)


def logit_kernel(
    back, tokens, cotangent, dispatch_in, combine_in, send, grad_low_out, slot_out, grad_slot_in
):
    slot_out[...] = back[:, 0].reshape(slot_out.shape)
    grad_slot_in[...] = back[:, 1].reshape(slot_out.shape)
    dispatch = dispatch_in[...]
    combine = combine_in[...]
    grad_combine = dot(cotangent[...], slot_out[...], ((1,), (1,)))
    grad_dispatch = dot(tokens[...], grad_slot_in[...], ((1,), (1,)))
    grad_logits = dispatch * (
        grad_dispatch - jnp.sum(dispatch * grad_dispatch, axis=0, keepdims=True)
    ) + combine * (grad_combine - jnp.sum(combine * grad_combine, axis=1, keepdims=True))
    grad_low = grad_logits.astype(LOW)
    grad_low_out[...] = grad_low
    terms = dot(grad_low, tokens[...], ((0,), (0,))).astype(LOW)
    send[...] = terms.reshape(send.shape)


def sum_kernel(terms, total):
    width = terms.shape[2]
    parts = terms[...].reshape(-1, 8, width).astype(jnp.float32)
    eight = jnp.sum(parts, axis=0)
    acc = eight[0:SLOTS_EXP]
    for i in range(1, 8 // SLOTS_EXP):
        acc = acc + eight[i * SLOTS_EXP : (i + 1) * SLOTS_EXP]
    total[...] = acc


VMEM = pl.BlockSpec(memory_space=pltpu.VMEM)
ANYWHERE = pl.BlockSpec(memory_space=pl.ANY)


def shaped(dtype, *shape):
    return jax.ShapeDtypeStruct(shape, dtype)


def local(tokens, slot_keys, weight_in, weight_out, cotangent):
    devices = device_count()
    length, width = tokens.shape[1:]
    inner = weight_in.shape[2]
    slots = devices * SLOTS_EXP
    tokens, cotangent = tokens[0], cotangent[0]
    first_weight, second_weight = weight_in[0], weight_out[0]
    pair_shape = (devices, SLOTS_EXP, width)
    twin_shape = (devices, 2, SLOTS_EXP, width)
    keys = exchange(jnp.broadcast_to(slot_keys[None], pair_shape))

    send, dispatch, combine, keys_all = pl.pallas_call(
        route_kernel,
        out_shape=[
            shaped(LOW, *twin_shape),
            shaped(jnp.float32, length, slots),
            shaped(jnp.float32, length, slots),
            shaped(LOW, slots, width),
        ],
        in_specs=[VMEM] * 3,
        out_specs=[VMEM] * 4,
        compiler_params=pltpu.CompilerParams(vmem_limit_bytes=32 * MIB),
        name="route",
    )(tokens, cotangent, keys)
    arrived = exchange(send)

    rows = arrived.shape[0] * SLOTS_EXP
    steps = inner // FF_BLOCK
    send, hidden, grads = pl.pallas_call(
        expert_kernel,
        out_shape=[
            shaped(LOW, *twin_shape),
            shaped(LOW, rows, inner),
            shaped(LOW, rows, width),
        ],
        in_specs=[VMEM, ANYWHERE, ANYWHERE],
        out_specs=[VMEM] * 3,
        scratch_shapes=[
            pltpu.VMEM((rows, width), LOW),
            pltpu.VMEM((rows, inner), LOW),
            pltpu.VMEM((width, inner), LOW),
            pltpu.VMEM((inner, width), LOW),
            pltpu.SemaphoreType.DMA((2, steps)),
        ],
        compiler_params=pltpu.CompilerParams(vmem_limit_bytes=60 * MIB),
        name="expert",
    )(arrived, first_weight, second_weight)
    back = exchange(send)
    grad_second = dot(hidden, grads, ((0,), (0,))).astype(LOW)

    send, grad_low, slot_out, grad_slot_in = pl.pallas_call(
        logit_kernel,
        out_shape=[
            shaped(LOW, *pair_shape),
            shaped(LOW, length, slots),
            shaped(LOW, slots, width),
            shaped(LOW, slots, width),
        ],
        in_specs=[VMEM] * 5,
        out_specs=[VMEM] * 4,
        compiler_params=pltpu.CompilerParams(vmem_limit_bytes=32 * MIB),
        name="logit",
    )(back, tokens, cotangent, dispatch, combine)
    terms = exchange(send)
    mixed_out = dot(combine.astype(LOW), slot_out, ((1,), (0,))).astype(LOW)
    through_slots = dot(dispatch.astype(LOW), grad_slot_in, ((1,), (0,)))
    through_keys = dot(grad_low, keys_all, ((1,), (0,)))
    grad_tokens = (through_slots + through_keys).astype(LOW)
    grad_keys = pl.pallas_call(
        sum_kernel,
        out_shape=shaped(jnp.float32, SLOTS_EXP, width),
        in_specs=[VMEM],
        out_specs=VMEM,
        compiler_params=pltpu.CompilerParams(vmem_limit_bytes=16 * MIB),
        name="total",
    )(terms)
    return (mixed_out[None], grad_tokens[None], grad_keys, grad_second[None])


def solution(mesh):
    in_specs = (
        P(AXES, None, None),
        P(AXES, None),
        P(AXES, None, None),
        P(AXES, None, None),
        P(AXES, None, None),
    )
    out_specs = (
        P(AXES, None, None),
        P(AXES, None, None),
        P(AXES, None),
        P(AXES, None, None),
    )
    return jax.shard_map(local, mesh=mesh, in_specs=in_specs, out_specs=out_specs, check_vma=False)
```

```python
import jax
import jax.numpy as jnp
from jax import lax
from jax.experimental import pallas as pl
from jax.experimental.pallas import tpu as pltpu
from jax.sharding import PartitionSpec as P

SLOTS_EXP = 2
AXES = ("dp", "mp")
LOW = jnp.bfloat16
FF_BLOCK = 512
D_BLOCK = 256
SEND_PARTS = 4
MIB = 1 << 20

inv_root_two = 0.7071067811865476
inv_root_tau = 0.3989422804014327


def gelu_pair(values):
    cumulative = 0.5 * (1.0 + lax.erf(values * inv_root_two))
    density = jnp.exp(-0.5 * values * values) * inv_root_tau
    return (values * cumulative, cumulative + values * density)


def device_count():
    return lax.axis_size(AXES)


def exchange(blocks):
    return lax.all_to_all(blocks, AXES, split_axis=0, concat_axis=0, tiled=True)


def dot(a, b, dims):
    return lax.dot_general(a, b, (dims, ((), ())), preferred_element_type=jnp.float32)


def softmax(values, axis):
    powers = jnp.exp(values - jnp.max(values, axis=axis, keepdims=True))
    return powers / jnp.sum(powers, axis=axis, keepdims=True)


def route_kernel(
    tokens, cotangent, keys, send, dispatch_out, combine_out, keys_hbm, keys_flat, sem
):
    pairs = keys.shape[0]
    slots, width = keys_flat.shape
    keys_flat[...] = keys[...].reshape(slots, width)
    keep = pltpu.make_async_copy(keys_flat, keys_hbm, sem)
    keep.start()
    logits = dot(tokens[...], keys_flat[...], ((1,), (1,)))
    dispatch = softmax(logits, 0)
    dispatch_out[...] = dispatch
    slots_in = dot(dispatch.astype(LOW), tokens[...], ((0,), (0,))).astype(LOW)
    send[:, 0] = slots_in.reshape(pairs, SLOTS_EXP, width)
    combine = softmax(logits, 1)
    combine_out[...] = combine
    grad_slot_out = dot(combine.astype(LOW), cotangent[...], ((0,), (0,))).astype(LOW)
    send[:, 1] = grad_slot_out.reshape(pairs, SLOTS_EXP, width)
    keep.wait()


def expert_kernel(arrived, first, second, send, hidden, grads, rows, grad_pre):
    width, inner = first.shape
    pairs = arrived.shape[0]
    rows[...] = arrived[:, 0].reshape(rows.shape)
    grads[...] = arrived[:, 1].reshape(rows.shape)
    for i in range(inner // FF_BLOCK):
        block = pl.ds(i * FF_BLOCK, FF_BLOCK)
        pre_act = dot(rows[...], first[:, block], ((1,), (0,)))
        grad_hidden = dot(grads[...], second[block, :], ((1,), (1,)))
        active, slope = gelu_pair(pre_act)
        hidden[:, block] = active.astype(LOW)
        grad_pre[:, block] = (grad_hidden * slope).astype(LOW)
    for j in range(width // D_BLOCK):
        block = pl.ds(j * D_BLOCK, D_BLOCK)
        out = dot(hidden[...], second[:, block], ((1,), (0,))).astype(LOW)
        send[:, 0, :, block] = out.reshape(pairs, SLOTS_EXP, D_BLOCK)
        back = dot(grad_pre[...], first[block, :], ((1,), (1,))).astype(LOW)
        send[:, 1, :, block] = back.reshape(pairs, SLOTS_EXP, D_BLOCK)


def logit_kernel(
    back,
    tokens,
    cotangent,
    dispatch_in,
    combine_in,
    send_hbm,
    grad_low_out,
    send,
    slot_out,
    grad_slot_in,
    sems,
):
    pairs, each, width = send.shape
    slot_out[...] = back[:, 0].reshape(slot_out.shape)
    grad_slot_in[...] = back[:, 1].reshape(slot_out.shape)
    dispatch = dispatch_in[...]
    combine = combine_in[...]
    grad_combine = dot(cotangent[...], slot_out[...], ((1,), (1,)))
    grad_dispatch = dot(tokens[...], grad_slot_in[...], ((1,), (1,)))
    grad_logits = dispatch * (
        grad_dispatch - jnp.sum(dispatch * grad_dispatch, axis=0, keepdims=True)
    ) + combine * (grad_combine - jnp.sum(combine * grad_combine, axis=1, keepdims=True))
    grad_low = grad_logits.astype(LOW)
    grad_low_out[...] = grad_low
    terms = dot(grad_low, tokens[...], ((0,), (0,))).astype(LOW)
    some = pairs // SEND_PARTS
    copies = []
    for j in range(SEND_PARTS):
        part = pl.ds(j * some, some)
        send[part] = terms[j * some * each : (j + 1) * some * each].reshape(some, each, width)
        copies.append(
            pltpu.make_async_copy(send.at[part], send_hbm.at[part], sems.at[j])
        )
        copies[-1].start()
    for copy in copies:
        copy.wait()


def finish_kernel(
    back, dispatch, combine, grad_low, keys, mixed_out, grad_tokens, slot_out, grad_slot_in
):
    slot_out[...] = back[:, 0].reshape(slot_out.shape)
    mixed_out[...] = dot(combine[...].astype(LOW), slot_out[...], ((1,), (0,))).astype(LOW)
    grad_slot_in[...] = back[:, 1].reshape(slot_out.shape)
    through_slots = dot(dispatch[...].astype(LOW), grad_slot_in[...], ((1,), (0,)))
    through_keys = dot(grad_low[...], keys[...], ((1,), (0,)))
    grad_tokens[...] = (through_slots + through_keys).astype(LOW)


def sum_kernel(terms, total):
    pairs, each, width = terms.shape
    owner = lax.broadcasted_iota(jnp.int32, (8, pairs * each), 0)
    slot = lax.broadcasted_iota(jnp.int32, (8, pairs * each), 1) % each
    chosen = jnp.where(owner == slot, 1.0, 0.0).astype(LOW)
    flat = terms[...].reshape(pairs * each, width)
    total[...] = dot(chosen, flat, ((1,), (0,)))[0:each]


def spread_kernel(keys, send):
    send[...] = jnp.broadcast_to(keys[...][None], send.shape)


BESIDE = pl.CostEstimate(flops=20_000_000_000, bytes_accessed=1_000_000, transcendentals=0)
VMEM = pl.BlockSpec(memory_space=pltpu.VMEM)
HBM = pl.BlockSpec(memory_space=pltpu.HBM)


def in_hbm(dtype, *shape):
    return pltpu.HBM(shape, dtype)


def shaped(dtype, *shape):
    return jax.ShapeDtypeStruct(shape, dtype)


def local(tokens, slot_keys, weight_in, weight_out, cotangent):
    devices = device_count()
    length, width = tokens.shape[1:]
    inner = weight_in.shape[2]
    slots = devices * SLOTS_EXP
    tokens, cotangent = tokens[0], cotangent[0]
    first_weight, second_weight = weight_in[0], weight_out[0]
    pair_shape = (devices, SLOTS_EXP, width)
    twin_shape = (devices, 2, SLOTS_EXP, width)
    send = pl.pallas_call(
        spread_kernel,
        out_shape=shaped(LOW, *pair_shape),
        in_specs=[VMEM],
        out_specs=VMEM,
        cost_estimate=BESIDE,
        compiler_params=pltpu.CompilerParams(vmem_limit_bytes=4 * MIB),
        name="spread",
    )(slot_keys)
    keys = exchange(send)

    send, dispatch, combine, keys_all = pl.pallas_call(
        route_kernel,
        out_shape=[
            shaped(LOW, *twin_shape),
            shaped(jnp.float32, length, slots),
            shaped(jnp.float32, length, slots),
            in_hbm(LOW, slots, width),
        ],
        in_specs=[VMEM] * 3,
        out_specs=[VMEM] * 3 + [HBM],
        scratch_shapes=[pltpu.VMEM((slots, width), LOW), pltpu.SemaphoreType.DMA],
        cost_estimate=BESIDE,
        compiler_params=pltpu.CompilerParams(vmem_limit_bytes=8 * MIB),
        name="route",
    )(tokens, cotangent, keys)
    arrived = exchange(send)

    rows = arrived.shape[0] * SLOTS_EXP
    send, hidden, grads = pl.pallas_call(
        expert_kernel,
        out_shape=[
            shaped(LOW, *twin_shape),
            shaped(LOW, rows, inner),
            shaped(LOW, rows, width),
        ],
        in_specs=[VMEM] * 3,
        out_specs=[VMEM] * 3,
        scratch_shapes=[
            pltpu.VMEM((rows, width), LOW),
            pltpu.VMEM((rows, inner), LOW),
        ],
        compiler_params=pltpu.CompilerParams(vmem_limit_bytes=10 * MIB),
        name="expert",
    )(arrived, first_weight, second_weight)
    back = exchange(send)
    grad_second = dot(hidden, grads, ((0,), (0,))).astype(LOW)

    send, grad_low = pl.pallas_call(
        logit_kernel,
        out_shape=[in_hbm(LOW, *pair_shape), shaped(LOW, length, slots)],
        in_specs=[VMEM] * 5,
        out_specs=[HBM, VMEM],
        scratch_shapes=[
            pltpu.VMEM(pair_shape, LOW),
            pltpu.VMEM((slots, width), LOW),
            pltpu.VMEM((slots, width), LOW),
            pltpu.SemaphoreType.DMA((SEND_PARTS,)),
        ],
        compiler_params=pltpu.CompilerParams(vmem_limit_bytes=8 * MIB),
        name="logit",
    )(back, tokens, cotangent, dispatch, combine)
    terms = exchange(send)
    mixed_out, grad_tokens = pl.pallas_call(
        finish_kernel,
        out_shape=[shaped(LOW, length, width)] * 2,
        in_specs=[VMEM] * 5,
        out_specs=[VMEM] * 2,
        scratch_shapes=[pltpu.VMEM((slots, width), LOW)] * 2,
        compiler_params=pltpu.CompilerParams(vmem_limit_bytes=8 * MIB),
        name="finish",
    )(back, dispatch, combine, grad_low, keys_all)
    grad_keys = pl.pallas_call(
        sum_kernel,
        out_shape=shaped(jnp.float32, SLOTS_EXP, width),
        in_specs=[VMEM],
        out_specs=VMEM,
        compiler_params=pltpu.CompilerParams(vmem_limit_bytes=4 * MIB),
        name="total",
    )(terms)
    return (mixed_out[None], grad_tokens[None], grad_keys, grad_second[None])


def solution(mesh):
    in_specs = (
        P(AXES, None, None),
        P(AXES, None),
        P(AXES, None, None),
        P(AXES, None, None),
        P(AXES, None, None),
    )
    out_specs = (
        P(AXES, None, None),
        P(AXES, None, None),
        P(AXES, None),
        P(AXES, None, None),
    )
    return jax.shard_map(local, mesh=mesh, in_specs=in_specs, out_specs=out_specs, check_vma=False)
```

```python
import jax
import jax.numpy as jnp
from jax import lax
from jax.experimental import pallas as pl
from jax.experimental.pallas import tpu as pltpu
from jax.sharding import Mesh
from jax.sharding import PartitionSpec as P

SLOTS_EXP = 2
ACROSS = ("dp", "chip")
AXES = ("dp", "chip", "core")
CORES = 2
LOW = jnp.bfloat16
FF_BLOCK = 512
D_BLOCK = 256
SEND_PARTS = 2
MIB = 1 << 20

inv_root_two = 0.7071067811865476
inv_root_tau = 0.3989422804014327


def gelu_pair(values):
    cumulative = 0.5 * (1.0 + lax.erf(values * inv_root_two))
    density = jnp.exp(-0.5 * values * values) * inv_root_tau
    return (values * cumulative, cumulative + values * density)


def device_count():
    return lax.axis_size(AXES)


def exchange(blocks, axes=AXES):
    return lax.all_to_all(blocks, axes, split_axis=0, concat_axis=0, tiled=True)


def swap_cores(block):
    return lax.ppermute(block, "core", [(0, 1), (1, 0)])


def core_index():
    return lax.axis_index("core")


def dot(a, b, dims):
    return lax.dot_general(a, b, (dims, ((), ())), preferred_element_type=jnp.float32)


def softmax(values, axis):
    powers = jnp.exp(values - jnp.max(values, axis=axis, keepdims=True))
    return powers / jnp.sum(powers, axis=axis, keepdims=True)


def route_kernel(
    core,
    tokens,
    cotangent,
    own,
    other,
    send,
    dispatch_out,
    combine_out,
    keys_hbm,
    keys,
    keys_flat,
    sem,
):
    pairs = send.shape[0]
    slots, width = keys_flat.shape
    keys[:, core[0]] = own[...]
    keys[:, CORES - 1 - core[0]] = other[...]
    keys_flat[...] = keys[...].reshape(slots, width)
    keep = pltpu.make_async_copy(keys_flat, keys_hbm, sem)
    keep.start()
    logits = dot(tokens[...], keys_flat[...], ((1,), (1,)))
    dispatch = softmax(logits, 0)
    dispatch_out[...] = dispatch
    slots_in = dot(dispatch.astype(LOW), tokens[...], ((0,), (0,))).astype(LOW)
    send[:, 0] = slots_in.reshape(pairs, SLOTS_EXP, width)
    combine = softmax(logits, 1)
    combine_out[...] = combine
    grad_slot_out = dot(combine.astype(LOW), cotangent[...], ((0,), (0,))).astype(LOW)
    send[:, 1] = grad_slot_out.reshape(pairs, SLOTS_EXP, width)
    keep.wait()


def expert_kernel(arrived, first, second, send, hidden, grads, rows, grad_pre):
    width, inner = first.shape
    pairs = arrived.shape[0]
    rows[...] = arrived[:, 0].reshape(rows.shape)
    grads[...] = arrived[:, 1].reshape(rows.shape)
    for i in range(inner // FF_BLOCK):
        block = pl.ds(i * FF_BLOCK, FF_BLOCK)
        pre_act = dot(rows[...], first[:, block], ((1,), (0,)))
        grad_hidden = dot(grads[...], second[block, :], ((1,), (1,)))
        active, slope = gelu_pair(pre_act)
        hidden[:, block] = active.astype(LOW)
        grad_pre[:, block] = (grad_hidden * slope).astype(LOW)
    for j in range(width // D_BLOCK):
        block = pl.ds(j * D_BLOCK, D_BLOCK)
        out = dot(hidden[...], second[:, block], ((1,), (0,))).astype(LOW)
        send[:, 0, :, block] = out.reshape(pairs, SLOTS_EXP, D_BLOCK)
        back = dot(grad_pre[...], first[block, :], ((1,), (1,))).astype(LOW)
        send[:, 1, :, block] = back.reshape(pairs, SLOTS_EXP, D_BLOCK)


def logit_kernel(
    core,
    back,
    tokens,
    cotangent,
    dispatch_in,
    combine_in,
    own,
    other,
    grad_low_hbm,
    terms,
    grad_low,
    slot_out,
    grad_slot_in,
    sem,
):
    slot_out[...] = back[:, 0].reshape(slot_out.shape)
    grad_slot_in[...] = back[:, 1].reshape(slot_out.shape)
    dispatch = dispatch_in[...]
    combine = combine_in[...]
    grad_combine = dot(cotangent[...], slot_out[...], ((1,), (1,)))
    grad_dispatch = dot(tokens[...], grad_slot_in[...], ((1,), (1,)))
    grad_logits = dispatch * (
        grad_dispatch - jnp.sum(dispatch * grad_dispatch, axis=0, keepdims=True)
    ) + combine * (grad_combine - jnp.sum(combine * grad_combine, axis=1, keepdims=True))
    grad_low[...] = grad_logits.astype(LOW)
    keep = pltpu.make_async_copy(grad_low, grad_low_hbm, sem)
    keep.start()
    terms[...] = dot(grad_low[...], tokens[...], ((0,), (0,))).astype(LOW).reshape(terms.shape)
    other[...] = terms[:, CORES - 1 - core[0]]
    own[...] = terms[:, core[0]]
    keep.wait()


def add_kernel(own, other, sums_hbm, sums, sems):
    some = sums.shape[0] // SEND_PARTS
    copies = []
    for j in range(SEND_PARTS):
        part = pl.ds(j * some, some)
        sums[part] = own[part] + other[part]
        copies.append(pltpu.make_async_copy(sums.at[part], sums_hbm.at[part], sems.at[j]))
        copies[j].start()
    for copy in copies:
        copy.wait()


def finish_kernel(
    back, dispatch, combine, grad_low, keys, mixed_out, grad_tokens, slot_out, grad_slot_in
):
    slot_out[...] = back[:, 0].reshape(slot_out.shape)
    mixed_out[...] = dot(combine[...].astype(LOW), slot_out[...], ((1,), (0,))).astype(LOW)
    grad_slot_in[...] = back[:, 1].reshape(slot_out.shape)
    through_slots = dot(dispatch[...].astype(LOW), grad_slot_in[...], ((1,), (0,)))
    through_keys = dot(grad_low[...], keys[...], ((1,), (0,)))
    grad_tokens[...] = (through_slots + through_keys).astype(LOW)


def sum_kernel(terms, total):
    pairs, each, width = terms.shape
    owner = lax.broadcasted_iota(jnp.int32, (8, pairs * each), 0)
    slot = lax.broadcasted_iota(jnp.int32, (8, pairs * each), 1) % each
    chosen = jnp.where(owner == slot, 1.0, 0.0).astype(LOW)
    flat = terms[...].reshape(pairs * each, width)
    total[...] = dot(chosen, flat, ((1,), (0,)))[0:each]


def spread_kernel(keys, send):
    send[...] = jnp.broadcast_to(keys[...][None], send.shape)


BESIDE = pl.CostEstimate(flops=20_000_000_000, bytes_accessed=1_000_000, transcendentals=0)
VMEM = pl.BlockSpec(memory_space=pltpu.VMEM)
SMEM = pl.BlockSpec(memory_space=pltpu.SMEM)
HBM = pl.BlockSpec(memory_space=pltpu.HBM)


def in_hbm(dtype, *shape):
    return pltpu.HBM(shape, dtype)


def shaped(dtype, *shape):
    return jax.ShapeDtypeStruct(shape, dtype)


def local(tokens, slot_keys, weight_in, weight_out, cotangent):
    devices = device_count()
    length, width = tokens.shape[1:]
    inner = weight_in.shape[2]
    slots = devices * SLOTS_EXP
    tokens, cotangent = tokens[0], cotangent[0]
    first_weight, second_weight = weight_in[0], weight_out[0]
    half_shape = (devices // CORES, SLOTS_EXP, width)
    quad_shape = (devices // CORES, CORES, SLOTS_EXP, width)
    core = core_index()[None]
    twin_shape = (devices, 2, SLOTS_EXP, width)
    send = pl.pallas_call(
        spread_kernel,
        out_shape=shaped(LOW, *half_shape),
        in_specs=[VMEM],
        out_specs=VMEM,
        cost_estimate=BESIDE,
        compiler_params=pltpu.CompilerParams(vmem_limit_bytes=4 * MIB),
        name="spread",
    )(slot_keys)
    own_keys = exchange(send, ACROSS)
    other_keys = swap_cores(own_keys)

    send, dispatch, combine, keys_all = pl.pallas_call(
        route_kernel,
        out_shape=[
            shaped(LOW, *twin_shape),
            shaped(jnp.float32, length, slots),
            shaped(jnp.float32, length, slots),
            in_hbm(LOW, slots, width),
        ],
        in_specs=[SMEM] + [VMEM] * 4,
        out_specs=[VMEM] * 3 + [HBM],
        scratch_shapes=[
            pltpu.VMEM(quad_shape, LOW),
            pltpu.VMEM((slots, width), LOW),
            pltpu.SemaphoreType.DMA,
        ],
        cost_estimate=BESIDE,
        compiler_params=pltpu.CompilerParams(vmem_limit_bytes=8 * MIB),
        name="route",
    )(core, tokens, cotangent, own_keys, other_keys)
    arrived = exchange(send)

    rows = arrived.shape[0] * SLOTS_EXP
    send, hidden, grads = pl.pallas_call(
        expert_kernel,
        out_shape=[
            shaped(LOW, *twin_shape),
            shaped(LOW, rows, inner),
            shaped(LOW, rows, width),
        ],
        in_specs=[VMEM] * 3,
        out_specs=[VMEM] * 3,
        scratch_shapes=[
            pltpu.VMEM((rows, width), LOW),
            pltpu.VMEM((rows, inner), LOW),
        ],
        compiler_params=pltpu.CompilerParams(vmem_limit_bytes=10 * MIB),
        name="expert",
    )(arrived, first_weight, second_weight)
    back = exchange(send)
    grad_second = dot(hidden, grads, ((0,), (0,))).astype(LOW)

    own_terms, other_terms, grad_low = pl.pallas_call(
        logit_kernel,
        out_shape=[
            shaped(LOW, *half_shape),
            shaped(LOW, *half_shape),
            in_hbm(LOW, length, slots),
        ],
        in_specs=[SMEM] + [VMEM] * 5,
        out_specs=[VMEM, VMEM, HBM],
        scratch_shapes=[
            pltpu.VMEM(quad_shape, LOW),
            pltpu.VMEM((length, slots), LOW),
            pltpu.VMEM((slots, width), LOW),
            pltpu.VMEM((slots, width), LOW),
            pltpu.SemaphoreType.DMA,
        ],
        compiler_params=pltpu.CompilerParams(vmem_limit_bytes=8 * MIB),
        name="logit",
    )(core, back, tokens, cotangent, dispatch, combine)
    send = pl.pallas_call(
        add_kernel,
        out_shape=in_hbm(LOW, *half_shape),
        in_specs=[VMEM] * 2,
        out_specs=HBM,
        scratch_shapes=[pltpu.VMEM(half_shape, LOW), pltpu.SemaphoreType.DMA((SEND_PARTS,))],
        compiler_params=pltpu.CompilerParams(vmem_limit_bytes=4 * MIB),
        name="add",
    )(own_terms, swap_cores(other_terms))
    terms = exchange(send, ACROSS)
    mixed_out, grad_tokens = pl.pallas_call(
        finish_kernel,
        out_shape=[shaped(LOW, length, width)] * 2,
        in_specs=[VMEM] * 5,
        out_specs=[VMEM] * 2,
        scratch_shapes=[pltpu.VMEM((slots, width), LOW)] * 2,
        compiler_params=pltpu.CompilerParams(vmem_limit_bytes=8 * MIB),
        name="finish",
    )(back, dispatch, combine, grad_low, keys_all)
    grad_keys = pl.pallas_call(
        sum_kernel,
        out_shape=shaped(jnp.float32, SLOTS_EXP, width),
        in_specs=[VMEM],
        out_specs=VMEM,
        compiler_params=pltpu.CompilerParams(vmem_limit_bytes=4 * MIB),
        name="total",
    )(terms)
    return (mixed_out[None], grad_tokens[None], grad_keys, grad_second[None])


def solution(mesh):
    groups, members = mesh.devices.shape
    mesh = Mesh(mesh.devices.reshape(groups, members // CORES, CORES), AXES)
    in_specs = (
        P(AXES, None, None),
        P(AXES, None),
        P(AXES, None, None),
        P(AXES, None, None),
        P(AXES, None, None),
    )
    out_specs = (
        P(AXES, None, None),
        P(AXES, None, None),
        P(AXES, None),
        P(AXES, None, None),
    )
    return jax.shard_map(local, mesh=mesh, in_specs=in_specs, out_specs=out_specs, check_vma=False)
```

```python
import jax
import jax.numpy as jnp
from jax import lax
from jax.experimental import pallas as pl
from jax.experimental.pallas import tpu as pltpu
from jax.sharding import Mesh
from jax.sharding import PartitionSpec as P

SLOTS_EXP = 2
ACROSS = ("dp", "chip")
AXES = ("dp", "chip", "core")
CORES = 2
LOW = jnp.bfloat16
FF_BLOCK = 512
D_BLOCK = 256
SEND_PARTS = 2
MIB = 1 << 20

inv_root_two = 0.7071067811865476
inv_root_tau = 0.3989422804014327


def gelu_pair(values):
    cumulative = 0.5 * (1.0 + lax.erf(values * inv_root_two))
    density = jnp.exp(-0.5 * values * values) * inv_root_tau
    return (values * cumulative, cumulative + values * density)


def device_count():
    return lax.axis_size(AXES)


def exchange(blocks, axes=AXES):
    return lax.all_to_all(blocks, axes, split_axis=0, concat_axis=0, tiled=True)


def swap_cores(block):
    return lax.ppermute(block, "core", [(0, 1), (1, 0)])


def core_index():
    return lax.axis_index("core")


def dot(a, b, dims):
    return lax.dot_general(a, b, (dims, ((), ())), preferred_element_type=jnp.float32)


def softmax(values, axis):
    powers = jnp.exp(values - jnp.max(values, axis=axis, keepdims=True))
    return powers / jnp.sum(powers, axis=axis, keepdims=True)


def route_kernel(
    core,
    tokens,
    cotangent,
    own,
    other,
    send,
    dispatch_out,
    combine_out,
    keys_hbm,
    keys,
    keys_flat,
    sem,
):
    pairs = send.shape[0]
    slots, width = keys_flat.shape
    keys[:, core[0]] = own[...]
    keys[:, CORES - 1 - core[0]] = other[...]
    keys_flat[...] = keys[...].reshape(slots, width)
    keep = pltpu.make_async_copy(keys_flat, keys_hbm, sem)
    keep.start()
    logits = dot(tokens[...], keys_flat[...], ((1,), (1,)))
    dispatch = softmax(logits, 0)
    dispatch_out[...] = dispatch
    slots_in = dot(dispatch.astype(LOW), tokens[...], ((0,), (0,))).astype(LOW)
    send[:, 0] = slots_in.reshape(pairs, SLOTS_EXP, width)
    combine = softmax(logits, 1)
    combine_out[...] = combine
    grad_slot_out = dot(combine.astype(LOW), cotangent[...], ((0,), (0,))).astype(LOW)
    send[:, 1] = grad_slot_out.reshape(pairs, SLOTS_EXP, width)
    keep.wait()


def expert_kernel(arrived, first, second, send, hidden, grads_hbm, rows, grads, grad_pre, sem):
    width, inner = first.shape
    pairs = arrived.shape[0]
    rows[...] = arrived[:, 0].reshape(rows.shape)
    for i in range(inner // FF_BLOCK):
        block = pl.ds(i * FF_BLOCK, FF_BLOCK)
        pre_act = dot(rows[...], first[:, block], ((1,), (0,)))
        if i == 0:
            grads[...] = arrived[:, 1].reshape(rows.shape)
            keep = pltpu.make_async_copy(grads, grads_hbm, sem)
            keep.start()
        grad_hidden = dot(grads[...], second[block, :], ((1,), (1,)))
        active, slope = gelu_pair(pre_act)
        hidden[:, block] = active.astype(LOW)
        grad_pre[:, block] = (grad_hidden * slope).astype(LOW)
    for j in range(width // D_BLOCK):
        block = pl.ds(j * D_BLOCK, D_BLOCK)
        out = dot(hidden[...], second[:, block], ((1,), (0,))).astype(LOW)
        send[:, 0, :, block] = out.reshape(pairs, SLOTS_EXP, D_BLOCK)
        back = dot(grad_pre[...], first[block, :], ((1,), (1,))).astype(LOW)
        send[:, 1, :, block] = back.reshape(pairs, SLOTS_EXP, D_BLOCK)
    keep.wait()


def logit_kernel(
    core,
    back,
    tokens,
    cotangent,
    dispatch_in,
    combine_in,
    own,
    other,
    grad_low_hbm,
    terms,
    grad_low,
    slot_out,
    grad_slot_in,
    sem,
):
    slot_out[...] = back[:, 0].reshape(slot_out.shape)
    grad_slot_in[...] = back[:, 1].reshape(slot_out.shape)
    dispatch = dispatch_in[...]
    combine = combine_in[...]
    grad_combine = dot(cotangent[...], slot_out[...], ((1,), (1,)))
    grad_dispatch = dot(tokens[...], grad_slot_in[...], ((1,), (1,)))
    grad_logits = dispatch * (
        grad_dispatch - jnp.sum(dispatch * grad_dispatch, axis=0, keepdims=True)
    ) + combine * (grad_combine - jnp.sum(combine * grad_combine, axis=1, keepdims=True))
    grad_low[...] = grad_logits.astype(LOW)
    keep = pltpu.make_async_copy(grad_low, grad_low_hbm, sem)
    keep.start()
    terms[...] = dot(grad_low[...], tokens[...], ((0,), (0,))).astype(LOW).reshape(terms.shape)
    other[...] = terms[:, CORES - 1 - core[0]]
    own[...] = terms[:, core[0]]
    keep.wait()


def add_kernel(own, other, sums_hbm, sums, sems):
    some = sums.shape[0] // SEND_PARTS
    copies = []
    for j in range(SEND_PARTS):
        part = pl.ds(j * some, some)
        sums[part] = own[part] + other[part]
        copies.append(pltpu.make_async_copy(sums.at[part], sums_hbm.at[part], sems.at[j]))
        copies[j].start()
    for copy in copies:
        copy.wait()


def finish_kernel(
    back,
    dispatch,
    combine,
    hidden,
    grad_low_hbm,
    keys_hbm,
    grads_hbm,
    mixed_hbm,
    grad_tokens_hbm,
    grad_second_hbm,
    slot_out,
    grad_slot_in,
    grad_low,
    keys,
    grads,
    mixed_out,
    grad_tokens,
    blocks,
    sems,
):
    arrivals = [
        pltpu.make_async_copy(grad_low_hbm, grad_low, sems.at[5]),
        pltpu.make_async_copy(keys_hbm, keys, sems.at[6]),
        pltpu.make_async_copy(grads_hbm, grads, sems.at[0]),
    ]
    for arrival in arrivals:
        arrival.start()
    slot_out[...] = back[:, 0].reshape(slot_out.shape)
    mixed_out[...] = dot(combine[...].astype(LOW), slot_out[...], ((1,), (0,))).astype(LOW)
    leave_mixed = pltpu.make_async_copy(mixed_out, mixed_hbm, sems.at[1])
    leave_mixed.start()
    grad_slot_in[...] = back[:, 1].reshape(slot_out.shape)
    through_slots = dot(dispatch[...].astype(LOW), grad_slot_in[...], ((1,), (0,)))
    arrivals[0].wait()
    arrivals[1].wait()
    through_keys = dot(grad_low[...], keys[...], ((1,), (0,)))
    grad_tokens[...] = (through_slots + through_keys).astype(LOW)
    leave_tokens = pltpu.make_async_copy(grad_tokens, grad_tokens_hbm, sems.at[2])
    leave_tokens.start()
    arrivals[2].wait()
    copies = []
    for i in range(hidden.shape[1] // FF_BLOCK):
        if i >= 2:
            copies[i - 2].wait()
        block = pl.ds(i * FF_BLOCK, FF_BLOCK)
        blocks[i % 2] = dot(hidden[:, block], grads[...], ((0,), (0,))).astype(LOW)
        copies.append(
            pltpu.make_async_copy(blocks.at[i % 2], grad_second_hbm.at[block], sems.at[3 + i % 2])
        )
        copies[i].start()
    for copy in (leave_mixed, leave_tokens, *copies[-2:]):
        copy.wait()


def sum_kernel(terms, total):
    pairs, each, width = terms.shape
    owner = lax.broadcasted_iota(jnp.int32, (8, pairs * each), 0)
    slot = lax.broadcasted_iota(jnp.int32, (8, pairs * each), 1) % each
    chosen = jnp.where(owner == slot, 1.0, 0.0).astype(LOW)
    flat = terms[...].reshape(pairs * each, width)
    total[...] = dot(chosen, flat, ((1,), (0,)))[0:each]


def spread_kernel(keys_hbm, send, keys, sem):
    copy = pltpu.make_async_copy(keys_hbm, keys, sem)
    copy.start()
    copy.wait()
    send[...] = jnp.broadcast_to(keys[...][None], send.shape)


BESIDE = pl.CostEstimate(flops=20_000_000_000, bytes_accessed=1_000_000, transcendentals=0)
VMEM = pl.BlockSpec(memory_space=pltpu.VMEM)
SMEM = pl.BlockSpec(memory_space=pltpu.SMEM)
HBM = pl.BlockSpec(memory_space=pltpu.HBM)


def in_hbm(dtype, *shape):
    return pltpu.HBM(shape, dtype)


def stay(array):
    return pltpu.with_memory_space_constraint(array, pltpu.HBM)


def shaped(dtype, *shape):
    return jax.ShapeDtypeStruct(shape, dtype)


def local(tokens, slot_keys, weight_in, weight_out, cotangent):
    devices = device_count()
    length, width = tokens.shape[1:]
    inner = weight_in.shape[2]
    slots = devices * SLOTS_EXP
    tokens, cotangent = tokens[0], cotangent[0]
    first_weight, second_weight = weight_in[0], weight_out[0]
    half_shape = (devices // CORES, SLOTS_EXP, width)
    quad_shape = (devices // CORES, CORES, SLOTS_EXP, width)
    core = core_index()[None]
    twin_shape = (devices, 2, SLOTS_EXP, width)
    send = pl.pallas_call(
        spread_kernel,
        out_shape=shaped(LOW, *half_shape),
        in_specs=[HBM],
        out_specs=VMEM,
        scratch_shapes=[pltpu.VMEM((SLOTS_EXP, width), LOW), pltpu.SemaphoreType.DMA],
        cost_estimate=BESIDE,
        compiler_params=pltpu.CompilerParams(vmem_limit_bytes=4 * MIB),
        name="spread",
    )(stay(slot_keys))
    own_keys = exchange(send, ACROSS)
    other_keys = swap_cores(own_keys)

    send, dispatch, combine, keys_all = pl.pallas_call(
        route_kernel,
        out_shape=[
            shaped(LOW, *twin_shape),
            shaped(jnp.float32, length, slots),
            shaped(jnp.float32, length, slots),
            in_hbm(LOW, slots, width),
        ],
        in_specs=[SMEM] + [VMEM] * 4,
        out_specs=[VMEM] * 3 + [HBM],
        scratch_shapes=[
            pltpu.VMEM(quad_shape, LOW),
            pltpu.VMEM((slots, width), LOW),
            pltpu.SemaphoreType.DMA,
        ],
        cost_estimate=BESIDE,
        compiler_params=pltpu.CompilerParams(vmem_limit_bytes=8 * MIB),
        name="route",
    )(core, tokens, cotangent, own_keys, other_keys)
    arrived = exchange(send)

    rows = arrived.shape[0] * SLOTS_EXP
    send, hidden, grads = pl.pallas_call(
        expert_kernel,
        out_shape=[
            shaped(LOW, *twin_shape),
            shaped(LOW, rows, inner),
            in_hbm(LOW, rows, width),
        ],
        in_specs=[VMEM] * 3,
        out_specs=[VMEM] * 2 + [HBM],
        scratch_shapes=[
            pltpu.VMEM((rows, width), LOW),
            pltpu.VMEM((rows, width), LOW),
            pltpu.VMEM((rows, inner), LOW),
            pltpu.SemaphoreType.DMA,
        ],
        compiler_params=pltpu.CompilerParams(vmem_limit_bytes=10 * MIB),
        name="expert",
    )(arrived, first_weight, second_weight)
    back = exchange(send)

    own_terms, other_terms, grad_low = pl.pallas_call(
        logit_kernel,
        out_shape=[
            shaped(LOW, *half_shape),
            shaped(LOW, *half_shape),
            in_hbm(LOW, length, slots),
        ],
        in_specs=[SMEM] + [VMEM] * 5,
        out_specs=[VMEM, VMEM, HBM],
        scratch_shapes=[
            pltpu.VMEM(quad_shape, LOW),
            pltpu.VMEM((length, slots), LOW),
            pltpu.VMEM((slots, width), LOW),
            pltpu.VMEM((slots, width), LOW),
            pltpu.SemaphoreType.DMA,
        ],
        compiler_params=pltpu.CompilerParams(vmem_limit_bytes=8 * MIB),
        name="logit",
    )(core, back, tokens, cotangent, dispatch, combine)
    send = pl.pallas_call(
        add_kernel,
        out_shape=in_hbm(LOW, *half_shape),
        in_specs=[VMEM] * 2,
        out_specs=HBM,
        scratch_shapes=[pltpu.VMEM(half_shape, LOW), pltpu.SemaphoreType.DMA((SEND_PARTS,))],
        compiler_params=pltpu.CompilerParams(vmem_limit_bytes=4 * MIB),
        name="add",
    )(own_terms, swap_cores(other_terms))
    terms = exchange(send, ACROSS)
    mixed_out, grad_tokens, grad_second = pl.pallas_call(
        finish_kernel,
        out_shape=[
            in_hbm(LOW, length, width),
            in_hbm(LOW, length, width),
            in_hbm(LOW, inner, width),
        ],
        in_specs=[VMEM] * 4 + [HBM] * 3,
        out_specs=[HBM] * 3,
        scratch_shapes=[
            pltpu.VMEM((slots, width), LOW),
            pltpu.VMEM((slots, width), LOW),
            pltpu.VMEM((length, slots), LOW),
            pltpu.VMEM((slots, width), LOW),
            pltpu.VMEM((rows, width), LOW),
            pltpu.VMEM((length, width), LOW),
            pltpu.VMEM((length, width), LOW),
            pltpu.VMEM((2, FF_BLOCK, width), LOW),
            pltpu.SemaphoreType.DMA((7,)),
        ],
        compiler_params=pltpu.CompilerParams(vmem_limit_bytes=16 * MIB),
        name="finish",
    )(back, dispatch, combine, hidden, stay(grad_low), stay(keys_all), stay(grads))
    grad_keys = pl.pallas_call(
        sum_kernel,
        out_shape=shaped(jnp.float32, SLOTS_EXP, width),
        in_specs=[VMEM],
        out_specs=VMEM,
        compiler_params=pltpu.CompilerParams(vmem_limit_bytes=4 * MIB),
        name="total",
    )(terms)
    return (mixed_out[None], grad_tokens[None], grad_keys, grad_second[None])


def solution(mesh):
    groups, members = mesh.devices.shape
    mesh = Mesh(mesh.devices.reshape(groups, members // CORES, CORES), AXES)
    in_specs = (
        P(AXES, None, None),
        P(AXES, None),
        P(AXES, None, None),
        P(AXES, None, None),
        P(AXES, None, None),
    )
    out_specs = (
        P(AXES, None, None),
        P(AXES, None, None),
        P(AXES, None),
        P(AXES, None, None),
    )
    return jax.shard_map(local, mesh=mesh, in_specs=in_specs, out_specs=out_specs, check_vma=False)
```

```python
import jax
import jax.numpy as jnp
from jax import lax
from jax.experimental import pallas as pl
from jax.experimental.pallas import tpu as pltpu
from jax.sharding import Mesh
from jax.sharding import PartitionSpec as P

SLOTS_EXP = 2
ACROSS = ("dp", "chip")
AXES = ("dp", "chip", "core")
CORES = 2
LOW = jnp.bfloat16
FF_BLOCK = 512
D_BLOCK = 256
MIB = 1 << 20

inv_root_two = 0.7071067811865476
inv_root_tau = 0.3989422804014327


def gelu_pair(values):
    cumulative = 0.5 * (1.0 + lax.erf(values * inv_root_two))
    density = jnp.exp(-0.5 * values * values) * inv_root_tau
    return (values * cumulative, cumulative + values * density)


def device_count():
    return lax.axis_size(AXES)


def exchange(blocks, axes=AXES):
    return lax.all_to_all(blocks, axes, split_axis=0, concat_axis=0, tiled=True)


def swap_cores(block):
    return lax.ppermute(block, "core", [(0, 1), (1, 0)])


def core_index():
    return lax.axis_index("core")


def dot(a, b, dims):
    return lax.dot_general(a, b, (dims, ((), ())), preferred_element_type=jnp.float32)


def softmax(values, axis):
    powers = jnp.exp(values - jnp.max(values, axis=axis, keepdims=True))
    return powers / jnp.sum(powers, axis=axis, keepdims=True)


def route_kernel(
    core,
    tokens,
    cotangent,
    own,
    other,
    send,
    dispatch_out,
    combine_out,
    keys_hbm,
    keys,
    keys_flat,
    sem,
):
    pairs = send.shape[0]
    slots, width = keys_flat.shape
    keys[:, core[0]] = own[...]
    keys[:, CORES - 1 - core[0]] = other[...]
    keys_flat[...] = keys[...].reshape(slots, width)
    keep = pltpu.make_async_copy(keys_flat, keys_hbm, sem)
    keep.start()
    logits = dot(tokens[...], keys_flat[...], ((1,), (1,)))
    dispatch = softmax(logits, 0)
    dispatch_out[...] = dispatch
    slots_in = dot(dispatch.astype(LOW), tokens[...], ((0,), (0,))).astype(LOW)
    send[:, 0] = slots_in.reshape(pairs, SLOTS_EXP, width)
    combine = softmax(logits, 1)
    combine_out[...] = combine
    grad_slot_out = dot(combine.astype(LOW), cotangent[...], ((0,), (0,))).astype(LOW)
    send[:, 1] = grad_slot_out.reshape(pairs, SLOTS_EXP, width)
    keep.wait()


def expert_kernel(arrived, first, second, send, hidden, grads_hbm, rows, grads, grad_pre, sem):
    width, inner = first.shape
    pairs = arrived.shape[0]
    rows[...] = arrived[:, 0].reshape(rows.shape)
    for i in range(inner // FF_BLOCK):
        block = pl.ds(i * FF_BLOCK, FF_BLOCK)
        pre_act = dot(rows[...], first[:, block], ((1,), (0,)))
        if i == 0:
            grads[...] = arrived[:, 1].reshape(rows.shape)
            keep = pltpu.make_async_copy(grads, grads_hbm, sem)
            keep.start()
        grad_hidden = dot(grads[...], second[block, :], ((1,), (1,)))
        active, slope = gelu_pair(pre_act)
        hidden[:, block] = active.astype(LOW)
        grad_pre[:, block] = (grad_hidden * slope).astype(LOW)
    for j in range(width // D_BLOCK):
        block = pl.ds(j * D_BLOCK, D_BLOCK)
        out = dot(hidden[...], second[:, block], ((1,), (0,))).astype(LOW)
        send[:, 0, :, block] = out.reshape(pairs, SLOTS_EXP, D_BLOCK)
        back = dot(grad_pre[...], first[block, :], ((1,), (1,))).astype(LOW)
        send[:, 1, :, block] = back.reshape(pairs, SLOTS_EXP, D_BLOCK)
    keep.wait()


def logit_kernel(
    core,
    back,
    tokens,
    cotangent,
    dispatch_in,
    combine_in,
    own,
    other,
    grad_low,
    terms,
    slot_out,
    grad_slot_in,
):
    slot_out[...] = back[:, 0].reshape(slot_out.shape)
    grad_slot_in[...] = back[:, 1].reshape(slot_out.shape)
    dispatch = dispatch_in[...]
    combine = combine_in[...]
    grad_combine = dot(cotangent[...], slot_out[...], ((1,), (1,)))
    grad_dispatch = dot(tokens[...], grad_slot_in[...], ((1,), (1,)))
    grad_logits = dispatch * (
        grad_dispatch - jnp.sum(dispatch * grad_dispatch, axis=0, keepdims=True)
    ) + combine * (grad_combine - jnp.sum(combine * grad_combine, axis=1, keepdims=True))
    grad_low[...] = grad_logits.astype(LOW)
    terms[...] = dot(grad_low[...], tokens[...], ((0,), (0,))).astype(LOW).reshape(terms.shape)
    other[...] = terms[:, CORES - 1 - core[0]]
    own[...] = terms[:, core[0]]


def finish_kernel(
    back,
    dispatch,
    combine,
    hidden,
    grad_low,
    keys_hbm,
    grads_hbm,
    mixed_hbm,
    grad_tokens_hbm,
    grad_second_hbm,
    slot_out,
    grad_slot_in,
    keys,
    grads,
    mixed_out,
    grad_tokens,
    blocks,
    sems,
):
    arrivals = [
        pltpu.make_async_copy(keys_hbm, keys, sems.at[5]),
        pltpu.make_async_copy(grads_hbm, grads, sems.at[0]),
    ]
    for arrival in arrivals:
        arrival.start()
    slot_out[...] = back[:, 0].reshape(slot_out.shape)
    mixed_out[...] = dot(combine[...].astype(LOW), slot_out[...], ((1,), (0,))).astype(LOW)
    leave_mixed = pltpu.make_async_copy(mixed_out, mixed_hbm, sems.at[1])
    leave_mixed.start()
    grad_slot_in[...] = back[:, 1].reshape(slot_out.shape)
    through_slots = dot(dispatch[...].astype(LOW), grad_slot_in[...], ((1,), (0,)))
    arrivals[0].wait()
    through_keys = dot(grad_low[...], keys[...], ((1,), (0,)))
    grad_tokens[...] = (through_slots + through_keys).astype(LOW)
    leave_tokens = pltpu.make_async_copy(grad_tokens, grad_tokens_hbm, sems.at[2])
    leave_tokens.start()
    arrivals[1].wait()
    copies = []
    for i in range(hidden.shape[1] // FF_BLOCK):
        if i >= 2:
            copies[i - 2].wait()
        block = pl.ds(i * FF_BLOCK, FF_BLOCK)
        blocks[i % 2] = dot(hidden[:, block], grads[...], ((0,), (0,))).astype(LOW)
        copies.append(
            pltpu.make_async_copy(blocks.at[i % 2], grad_second_hbm.at[block], sems.at[3 + i % 2])
        )
        copies[i].start()
    for copy in (leave_mixed, leave_tokens, *copies[-2:]):
        copy.wait()


def spread_kernel(keys_hbm, send, keys, sem):
    copy = pltpu.make_async_copy(keys_hbm, keys, sem)
    copy.start()
    copy.wait()
    send[...] = jnp.broadcast_to(keys[...][None], send.shape)


BESIDE = pl.CostEstimate(flops=20_000_000_000, bytes_accessed=1_000_000, transcendentals=0)
VMEM = pl.BlockSpec(memory_space=pltpu.VMEM)
SMEM = pl.BlockSpec(memory_space=pltpu.SMEM)
HBM = pl.BlockSpec(memory_space=pltpu.HBM)


def in_hbm(dtype, *shape):
    return pltpu.HBM(shape, dtype)


def stay(array):
    return pltpu.with_memory_space_constraint(array, pltpu.HBM)


def stay_near(array):
    return pltpu.with_memory_space_constraint(array, pltpu.VMEM)


def shaped(dtype, *shape):
    return jax.ShapeDtypeStruct(shape, dtype)


def local(tokens, slot_keys, weight_in, weight_out, cotangent):
    devices = device_count()
    length, width = tokens.shape[1:]
    inner = weight_in.shape[2]
    slots = devices * SLOTS_EXP
    tokens, cotangent = tokens[0], cotangent[0]
    first_weight, second_weight = weight_in[0], weight_out[0]
    half_shape = (devices // CORES, SLOTS_EXP, width)
    quad_shape = (devices // CORES, CORES, SLOTS_EXP, width)
    core = core_index()[None]
    twin_shape = (devices, 2, SLOTS_EXP, width)
    send = pl.pallas_call(
        spread_kernel,
        out_shape=shaped(LOW, *half_shape),
        in_specs=[HBM],
        out_specs=VMEM,
        scratch_shapes=[pltpu.VMEM((SLOTS_EXP, width), LOW), pltpu.SemaphoreType.DMA],
        cost_estimate=BESIDE,
        compiler_params=pltpu.CompilerParams(vmem_limit_bytes=4 * MIB),
        name="spread",
    )(stay(slot_keys))
    own_keys = exchange(send, ACROSS)
    other_keys = swap_cores(own_keys)

    send, dispatch, combine, keys_all = pl.pallas_call(
        route_kernel,
        out_shape=[
            shaped(LOW, *twin_shape),
            shaped(jnp.float32, length, slots),
            shaped(jnp.float32, length, slots),
            in_hbm(LOW, slots, width),
        ],
        in_specs=[SMEM] + [VMEM] * 4,
        out_specs=[VMEM] * 3 + [HBM],
        scratch_shapes=[
            pltpu.VMEM(quad_shape, LOW),
            pltpu.VMEM((slots, width), LOW),
            pltpu.SemaphoreType.DMA,
        ],
        cost_estimate=BESIDE,
        compiler_params=pltpu.CompilerParams(vmem_limit_bytes=8 * MIB),
        name="route",
    )(core, tokens, cotangent, own_keys, other_keys)
    arrived = exchange(send)

    rows = arrived.shape[0] * SLOTS_EXP
    send, hidden, grads = pl.pallas_call(
        expert_kernel,
        out_shape=[
            shaped(LOW, *twin_shape),
            shaped(LOW, rows, inner),
            in_hbm(LOW, rows, width),
        ],
        in_specs=[VMEM] * 3,
        out_specs=[VMEM] * 2 + [HBM],
        scratch_shapes=[
            pltpu.VMEM((rows, width), LOW),
            pltpu.VMEM((rows, width), LOW),
            pltpu.VMEM((rows, inner), LOW),
            pltpu.SemaphoreType.DMA,
        ],
        compiler_params=pltpu.CompilerParams(vmem_limit_bytes=10 * MIB),
        name="expert",
    )(arrived, first_weight, second_weight)
    back = exchange(send)

    own_terms, other_terms, grad_low = pl.pallas_call(
        logit_kernel,
        out_shape=[
            shaped(LOW, *half_shape),
            shaped(LOW, *half_shape),
            pltpu.VMEM((length, slots), LOW),
        ],
        in_specs=[SMEM] + [VMEM] * 5,
        out_specs=[VMEM] * 3,
        scratch_shapes=[
            pltpu.VMEM(quad_shape, LOW),
            pltpu.VMEM((slots, width), LOW),
            pltpu.VMEM((slots, width), LOW),
        ],
        compiler_params=pltpu.CompilerParams(vmem_limit_bytes=8 * MIB),
        name="logit",
    )(core, back, tokens, cotangent, dispatch, combine)
    send = own_terms + swap_cores(other_terms)
    terms = exchange(send, ACROSS)
    mixed_out, grad_tokens, grad_second = pl.pallas_call(
        finish_kernel,
        out_shape=[
            in_hbm(LOW, length, width),
            in_hbm(LOW, length, width),
            in_hbm(LOW, inner, width),
        ],
        in_specs=[VMEM] * 5 + [HBM] * 2,
        out_specs=[HBM] * 3,
        scratch_shapes=[
            pltpu.VMEM((slots, width), LOW),
            pltpu.VMEM((slots, width), LOW),
            pltpu.VMEM((slots, width), LOW),
            pltpu.VMEM((rows, width), LOW),
            pltpu.VMEM((length, width), LOW),
            pltpu.VMEM((length, width), LOW),
            pltpu.VMEM((2, FF_BLOCK, width), LOW),
            pltpu.SemaphoreType.DMA((6,)),
        ],
        compiler_params=pltpu.CompilerParams(vmem_limit_bytes=16 * MIB),
        name="finish",
    )(back, dispatch, combine, hidden, stay_near(grad_low), stay(keys_all), stay(grads))
    grad_keys = jnp.sum(terms.astype(jnp.float32), axis=0)
    return (mixed_out[None], grad_tokens[None], grad_keys, grad_second[None])


def solution(mesh):
    groups, members = mesh.devices.shape
    mesh = Mesh(mesh.devices.reshape(groups, members // CORES, CORES), AXES)
    in_specs = (
        P(AXES, None, None),
        P(AXES, None),
        P(AXES, None, None),
        P(AXES, None, None),
        P(AXES, None, None),
    )
    out_specs = (
        P(AXES, None, None),
        P(AXES, None, None),
        P(AXES, None),
        P(AXES, None, None),
    )
    return jax.shard_map(local, mesh=mesh, in_specs=in_specs, out_specs=out_specs, check_vma=False)
```

```python
import jax
import jax.numpy as jnp
from jax import lax
from jax.experimental import pallas as pl
from jax.experimental.pallas import tpu as pltpu
from jax.sharding import Mesh
from jax.sharding import PartitionSpec as P

SLOTS_EXP = 2
ACROSS = ("dp", "chip")
AXES = ("dp", "chip", "core")
CORES = 2
LOW = jnp.bfloat16
FF_BLOCK = 512
D_BLOCK = 256
SEND_PARTS = 2
MIB = 1 << 20

inv_root_two = 0.7071067811865476
inv_root_tau = 0.3989422804014327


def gelu_pair(values):
    cumulative = 0.5 * (1.0 + lax.erf(values * inv_root_two))
    density = jnp.exp(-0.5 * values * values) * inv_root_tau
    return (values * cumulative, cumulative + values * density)


def device_count():
    return lax.axis_size(AXES)


def exchange(blocks, axes=AXES):
    return lax.all_to_all(blocks, axes, split_axis=0, concat_axis=0, tiled=True)


def swap_cores(block):
    return lax.ppermute(block, "core", [(0, 1), (1, 0)])


def core_index():
    return lax.axis_index("core")


def dot(a, b, dims):
    return lax.dot_general(a, b, (dims, ((), ())), preferred_element_type=jnp.float32)


def softmax(values, axis):
    powers = jnp.exp(values - jnp.max(values, axis=axis, keepdims=True))
    return powers / jnp.sum(powers, axis=axis, keepdims=True)


def route_kernel(
    core,
    tokens,
    cotangent,
    own,
    other,
    send,
    dispatch_out,
    combine_out,
    keys_hbm,
    keys,
    keys_flat,
    sem,
):
    pairs = send.shape[0]
    slots, width = keys_flat.shape
    keys[:, core[0]] = own[...]
    keys[:, CORES - 1 - core[0]] = other[...]
    keys_flat[...] = keys[...].reshape(slots, width)
    keep = pltpu.make_async_copy(keys_flat, keys_hbm, sem)
    keep.start()
    logits = dot(tokens[...], keys_flat[...], ((1,), (1,)))
    dispatch = softmax(logits, 0)
    dispatch_out[...] = dispatch
    slots_in = dot(dispatch.astype(LOW), tokens[...], ((0,), (0,))).astype(LOW)
    send[:, 0] = slots_in.reshape(pairs, SLOTS_EXP, width)
    combine = softmax(logits, 1)
    combine_out[...] = combine
    grad_slot_out = dot(combine.astype(LOW), cotangent[...], ((0,), (0,))).astype(LOW)
    send[:, 1] = grad_slot_out.reshape(pairs, SLOTS_EXP, width)
    keep.wait()


def expert_kernel(arrived, first, second, send, hidden, grads_hbm, rows, grads, grad_pre, sem):
    width, inner = first.shape
    pairs = arrived.shape[0]
    rows[...] = arrived[:, 0].reshape(rows.shape)
    for i in range(inner // FF_BLOCK):
        block = pl.ds(i * FF_BLOCK, FF_BLOCK)
        pre_act = dot(rows[...], first[:, block], ((1,), (0,)))
        if i == 0:
            grads[...] = arrived[:, 1].reshape(rows.shape)
            keep = pltpu.make_async_copy(grads, grads_hbm, sem)
            keep.start()
        grad_hidden = dot(grads[...], second[block, :], ((1,), (1,)))
        active, slope = gelu_pair(pre_act)
        hidden[:, block] = active.astype(LOW)
        grad_pre[:, block] = (grad_hidden * slope).astype(LOW)
    for j in range(width // D_BLOCK):
        block = pl.ds(j * D_BLOCK, D_BLOCK)
        out = dot(hidden[...], second[:, block], ((1,), (0,))).astype(LOW)
        send[:, 0, :, block] = out.reshape(pairs, SLOTS_EXP, D_BLOCK)
        back = dot(grad_pre[...], first[block, :], ((1,), (1,))).astype(LOW)
        send[:, 1, :, block] = back.reshape(pairs, SLOTS_EXP, D_BLOCK)
    keep.wait()


def logit_kernel(
    core,
    back,
    tokens,
    cotangent,
    dispatch_in,
    combine_in,
    own,
    other,
    grad_low,
    terms,
    slot_out,
    grad_slot_in,
):
    slot_out[...] = back[:, 0].reshape(slot_out.shape)
    grad_slot_in[...] = back[:, 1].reshape(slot_out.shape)
    dispatch = dispatch_in[...]
    combine = combine_in[...]
    grad_combine = dot(cotangent[...], slot_out[...], ((1,), (1,)))
    grad_dispatch = dot(tokens[...], grad_slot_in[...], ((1,), (1,)))
    grad_logits = dispatch * (
        grad_dispatch - jnp.sum(dispatch * grad_dispatch, axis=0, keepdims=True)
    ) + combine * (grad_combine - jnp.sum(combine * grad_combine, axis=1, keepdims=True))
    grad_low[...] = grad_logits.astype(LOW)
    terms[...] = dot(grad_low[...], tokens[...], ((0,), (0,))).astype(LOW).reshape(terms.shape)
    other[...] = terms[:, CORES - 1 - core[0]]
    own[...] = terms[:, core[0]]


def add_kernel(own, other, grad_low, sums_hbm, grad_low_hbm, sums, sems):
    some = sums.shape[0] // SEND_PARTS
    keep = pltpu.make_async_copy(grad_low, grad_low_hbm, sems.at[SEND_PARTS])
    keep.start()
    copies = [keep]
    for j in range(SEND_PARTS):
        part = pl.ds(j * some, some)
        sums[part] = own[part] + other[part]
        copies.append(pltpu.make_async_copy(sums.at[part], sums_hbm.at[part], sems.at[j]))
        copies[-1].start()
    for copy in copies:
        copy.wait()


def finish_kernel(
    back,
    dispatch,
    combine,
    hidden,
    grad_low_hbm,
    keys_hbm,
    grads_hbm,
    mixed_hbm,
    grad_tokens_hbm,
    grad_second_hbm,
    slot_out,
    grad_slot_in,
    grad_low,
    keys,
    grads,
    mixed_out,
    grad_tokens,
    blocks,
    sems,
):
    arrivals = [
        pltpu.make_async_copy(grad_low_hbm, grad_low, sems.at[5]),
        pltpu.make_async_copy(keys_hbm, keys, sems.at[6]),
        pltpu.make_async_copy(grads_hbm, grads, sems.at[0]),
    ]
    for arrival in arrivals:
        arrival.start()
    slot_out[...] = back[:, 0].reshape(slot_out.shape)
    mixed_out[...] = dot(combine[...].astype(LOW), slot_out[...], ((1,), (0,))).astype(LOW)
    leave_mixed = pltpu.make_async_copy(mixed_out, mixed_hbm, sems.at[1])
    leave_mixed.start()
    grad_slot_in[...] = back[:, 1].reshape(slot_out.shape)
    through_slots = dot(dispatch[...].astype(LOW), grad_slot_in[...], ((1,), (0,)))
    arrivals[0].wait()
    arrivals[1].wait()
    through_keys = dot(grad_low[...], keys[...], ((1,), (0,)))
    grad_tokens[...] = (through_slots + through_keys).astype(LOW)
    leave_tokens = pltpu.make_async_copy(grad_tokens, grad_tokens_hbm, sems.at[2])
    leave_tokens.start()
    arrivals[2].wait()
    copies = []
    for i in range(hidden.shape[1] // FF_BLOCK):
        if i >= 2:
            copies[i - 2].wait()
        block = pl.ds(i * FF_BLOCK, FF_BLOCK)
        blocks[i % 2] = dot(hidden[:, block], grads[...], ((0,), (0,))).astype(LOW)
        copies.append(
            pltpu.make_async_copy(blocks.at[i % 2], grad_second_hbm.at[block], sems.at[3 + i % 2])
        )
        copies[i].start()
    for copy in (leave_mixed, leave_tokens, *copies[-2:]):
        copy.wait()


def sum_kernel(terms, total):
    pairs, each, width = terms.shape
    owner = lax.broadcasted_iota(jnp.int32, (8, pairs * each), 0)
    slot = lax.broadcasted_iota(jnp.int32, (8, pairs * each), 1) % each
    chosen = jnp.where(owner == slot, 1.0, 0.0).astype(LOW)
    flat = terms[...].reshape(pairs * each, width)
    total[...] = dot(chosen, flat, ((1,), (0,)))[0:each]


def spread_kernel(keys_hbm, send, keys, sem):
    copy = pltpu.make_async_copy(keys_hbm, keys, sem)
    copy.start()
    copy.wait()
    send[...] = jnp.broadcast_to(keys[...][None], send.shape)


BESIDE = pl.CostEstimate(flops=20_000_000_000, bytes_accessed=1_000_000, transcendentals=0)
VMEM = pl.BlockSpec(memory_space=pltpu.VMEM)
SMEM = pl.BlockSpec(memory_space=pltpu.SMEM)
HBM = pl.BlockSpec(memory_space=pltpu.HBM)


def in_hbm(dtype, *shape):
    return pltpu.HBM(shape, dtype)


def stay(array):
    return pltpu.with_memory_space_constraint(array, pltpu.HBM)


def shaped(dtype, *shape):
    return jax.ShapeDtypeStruct(shape, dtype)


def local(tokens, slot_keys, weight_in, weight_out, cotangent):
    devices = device_count()
    length, width = tokens.shape[1:]
    inner = weight_in.shape[2]
    slots = devices * SLOTS_EXP
    tokens, cotangent = tokens[0], cotangent[0]
    first_weight, second_weight = weight_in[0], weight_out[0]
    half_shape = (devices // CORES, SLOTS_EXP, width)
    quad_shape = (devices // CORES, CORES, SLOTS_EXP, width)
    core = core_index()[None]
    twin_shape = (devices, 2, SLOTS_EXP, width)
    send = pl.pallas_call(
        spread_kernel,
        out_shape=shaped(LOW, *half_shape),
        in_specs=[HBM],
        out_specs=VMEM,
        scratch_shapes=[pltpu.VMEM((SLOTS_EXP, width), LOW), pltpu.SemaphoreType.DMA],
        cost_estimate=BESIDE,
        compiler_params=pltpu.CompilerParams(vmem_limit_bytes=4 * MIB),
        name="spread",
    )(stay(slot_keys))
    own_keys = exchange(send, ACROSS)
    other_keys = swap_cores(own_keys)

    send, dispatch, combine, keys_all = pl.pallas_call(
        route_kernel,
        out_shape=[
            shaped(LOW, *twin_shape),
            shaped(jnp.float32, length, slots),
            shaped(jnp.float32, length, slots),
            in_hbm(LOW, slots, width),
        ],
        in_specs=[SMEM] + [VMEM] * 4,
        out_specs=[VMEM] * 3 + [HBM],
        scratch_shapes=[
            pltpu.VMEM(quad_shape, LOW),
            pltpu.VMEM((slots, width), LOW),
            pltpu.SemaphoreType.DMA,
        ],
        cost_estimate=BESIDE,
        compiler_params=pltpu.CompilerParams(vmem_limit_bytes=8 * MIB),
        name="route",
    )(core, tokens, cotangent, own_keys, other_keys)
    arrived = exchange(send)

    rows = arrived.shape[0] * SLOTS_EXP
    send, hidden, grads = pl.pallas_call(
        expert_kernel,
        out_shape=[
            shaped(LOW, *twin_shape),
            shaped(LOW, rows, inner),
            in_hbm(LOW, rows, width),
        ],
        in_specs=[VMEM] * 3,
        out_specs=[VMEM] * 2 + [HBM],
        scratch_shapes=[
            pltpu.VMEM((rows, width), LOW),
            pltpu.VMEM((rows, width), LOW),
            pltpu.VMEM((rows, inner), LOW),
            pltpu.SemaphoreType.DMA,
        ],
        compiler_params=pltpu.CompilerParams(vmem_limit_bytes=10 * MIB),
        name="expert",
    )(arrived, first_weight, second_weight)
    back = exchange(send)

    own_terms, other_terms, grad_low = pl.pallas_call(
        logit_kernel,
        out_shape=[
            shaped(LOW, *half_shape),
            shaped(LOW, *half_shape),
            shaped(LOW, length, slots),
        ],
        in_specs=[SMEM] + [VMEM] * 5,
        out_specs=[VMEM] * 3,
        scratch_shapes=[
            pltpu.VMEM(quad_shape, LOW),
            pltpu.VMEM((slots, width), LOW),
            pltpu.VMEM((slots, width), LOW),
        ],
        compiler_params=pltpu.CompilerParams(vmem_limit_bytes=8 * MIB),
        name="logit",
    )(core, back, tokens, cotangent, dispatch, combine)
    send, grad_low = pl.pallas_call(
        add_kernel,
        out_shape=[in_hbm(LOW, *half_shape), in_hbm(LOW, length, slots)],
        in_specs=[VMEM] * 3,
        out_specs=[HBM] * 2,
        scratch_shapes=[pltpu.VMEM(half_shape, LOW), pltpu.SemaphoreType.DMA((SEND_PARTS + 1,))],
        compiler_params=pltpu.CompilerParams(vmem_limit_bytes=4 * MIB),
        name="add",
    )(own_terms, swap_cores(other_terms), grad_low)
    terms = exchange(send, ACROSS)
    mixed_out, grad_tokens, grad_second = pl.pallas_call(
        finish_kernel,
        out_shape=[
            in_hbm(LOW, length, width),
            in_hbm(LOW, length, width),
            in_hbm(LOW, inner, width),
        ],
        in_specs=[VMEM] * 4 + [HBM] * 3,
        out_specs=[HBM] * 3,
        scratch_shapes=[
            pltpu.VMEM((slots, width), LOW),
            pltpu.VMEM((slots, width), LOW),
            pltpu.VMEM((length, slots), LOW),
            pltpu.VMEM((slots, width), LOW),
            pltpu.VMEM((rows, width), LOW),
            pltpu.VMEM((length, width), LOW),
            pltpu.VMEM((length, width), LOW),
            pltpu.VMEM((2, FF_BLOCK, width), LOW),
            pltpu.SemaphoreType.DMA((7,)),
        ],
        compiler_params=pltpu.CompilerParams(vmem_limit_bytes=16 * MIB),
        name="finish",
    )(back, dispatch, combine, hidden, stay(grad_low), stay(keys_all), stay(grads))
    grad_keys = pl.pallas_call(
        sum_kernel,
        out_shape=shaped(jnp.float32, SLOTS_EXP, width),
        in_specs=[VMEM],
        out_specs=VMEM,
        compiler_params=pltpu.CompilerParams(vmem_limit_bytes=4 * MIB),
        name="total",
    )(terms)
    return (mixed_out[None], grad_tokens[None], grad_keys, grad_second[None])


def solution(mesh):
    groups, members = mesh.devices.shape
    mesh = Mesh(mesh.devices.reshape(groups, members // CORES, CORES), AXES)
    in_specs = (
        P(AXES, None, None),
        P(AXES, None),
        P(AXES, None, None),
        P(AXES, None, None),
        P(AXES, None, None),
    )
    out_specs = (
        P(AXES, None, None),
        P(AXES, None, None),
        P(AXES, None),
        P(AXES, None, None),
    )
    return jax.shard_map(local, mesh=mesh, in_specs=in_specs, out_specs=out_specs, check_vma=False)
```
